512 devices in a mesh: dp: 32 (over x_lo, y, core), block: 16 (over z, x_hi).
Axes of the slice: x: 4 (x_hi: 2, x_lo: 2; x = x_hi * 2 + x_lo), y: 8, z: 8, core: 2. Of those that a mesh axis runs over, the one named last changes fastest.
Arguments:
- act_rows: bfloat16 [2, 4, 512, 5120], P(None, None, 'dp', 'block'), may hold values from -6 to 6
- grad_rows: bfloat16 [2, 4, 512, 5120], P(None, None, 'dp', 'block'), may hold values from -6 to 6
- eig_act: bfloat16 [2, 16, 320, 320], P(None, 'block'), may hold values from -0.3125 to 0.3125
- eig_grad: bfloat16 [2, 16, 320, 320], P(None, 'block'), may hold values from -0.3125 to 0.3125
- precond: bfloat16 [2, 5120, 10240], P(None, 'block', 'dp'), may hold values from -0.0008544922 to 0.0008544922
- lengths: int32 [4], replicated, may hold values from 128 to 512
Outputs:
- token_influence: float32 [2, 4, 512], P(None, None, ('dp', 'block'))
The draws below stay inside these ranges and needn't reach their ends.
All inputs are finite; a program needn't handle non-finite values.
Results may differ from the reference program's by a relative error of at most 0.007.
Values may be sent and summed in bfloat16 or wider, within the bound.
No kernel may reach another device: no remote copies, remote signals or barrier semaphores. Data moves between devices by JAX's collectives and lax.ppermute only.
A program may use at most 64 MiB of HBM per device.

```python
import jax
import jax.numpy as jnp

D = 5120
BS = 320
NB = 16
LAYERS = 2
QUERIES = 2
SEQ_LEN = 512
SEQS = 4


def plant(entries, key, smallest, high):
    longest = entries.shape.index(max(entries.shape))
    spots = []
    for shift in (0, 1):
        where = [jax.random.randint(jax.random.fold_in(key, axis), (), 0, length) for axis, length in enumerate(entries.shape)]
        where[longest] = (where[longest] + shift) % entries.shape[longest]
        spots.append(tuple(where))
    return entries.at[spots[0]].set(smallest).at[spots[1]].set(high)


def levels(own_key, shape, split, least, high):
    def one(dim, shards_of):
        draws = jax.random.uniform(jax.random.fold_in(jax.random.fold_in(own_key, 6), dim), (shards_of,), jnp.float32, least / len(split), high / len(split))
        return jnp.repeat(jnp.exp(draws), shape[dim] // shards_of).reshape((-1,) + (1,) * (len(shape) - dim - 1))

    level = one(*split[0])
    for cut in split[1:]:
        level = level * one(*cut)
    return level


def gaussian(key, extent, width, bound, split=(), kind=jnp.bfloat16):
    factor_of = levels(key, extent, split, -0.22, 0.18) if split else 1.0
    values = jax.random.normal(key, extent, jnp.float32) * width * factor_of
    return jnp.minimum(jnp.maximum(values, -bound), bound).astype(kind)


def setup_inputs(seed: int = 0) -> dict:
    key_list = jax.random.split(jax.random.key(seed), 7)
    act_rows = gaussian(key_list[0], (LAYERS, SEQS, SEQ_LEN, D), 1.0, 6.0, ((2, 32), (3, 16)))
    grad_rows = gaussian(key_list[1], (LAYERS, SEQS, SEQ_LEN, D), 1.0, 6.0, ((2, 32), (3, 16)))
    eig_act = gaussian(key_list[2], (LAYERS, NB, BS, BS), BS ** -0.5, 0.3125, ((1, 16),))
    eig_grad = gaussian(key_list[3], (LAYERS, NB, BS, BS), BS ** -0.5, 0.3125, ((1, 16),))
    precond = gaussian(key_list[4], (QUERIES, D, LAYERS * D), (LAYERS * D * D) ** -0.5, 0.0008544922, ((1, 16), (2, 32)))
    lengths = plant(jax.random.randint(key_list[5], (SEQS,), SEQ_LEN // 4, SEQ_LEN + 1), jax.random.fold_in(key_list[5], 1), SEQ_LEN // 4, SEQ_LEN).astype(jnp.int32)
    return dict(act_rows=act_rows, grad_rows=grad_rows, eig_act=eig_act, eig_grad=eig_grad, precond=precond, lengths=lengths)


def rotate(rows, basis):
    layer_count, seq_count, seq_span, width_all = rows.shape
    block_count, block_size = basis.shape[1], basis.shape[2]
    blocked = rows.reshape(layer_count, seq_count * seq_span, block_count, block_size).astype(jnp.float32)
    turned = jnp.einsum("ltnr,lnrc->ltnc", blocked, basis.astype(jnp.float32))
    return turned.astype(jnp.bfloat16).reshape(rows.shape)


def reference(act_rows, grad_rows, eig_act, eig_grad, precond, lengths):
    act_rot = rotate(act_rows, eig_act)
    grad_rot = rotate(grad_rows, eig_grad)
    tokens = SEQS * SEQ_LEN
    scores = []
    for query_index in range(QUERIES):
        running = jnp.zeros((tokens,), jnp.float32)
        for layer_index in range(LAYERS):
            query_table = precond[query_index, :, layer_index * D:(layer_index + 1) * D]
            act_flat = act_rot[layer_index].reshape(tokens, D)
            grad_flat = grad_rot[layer_index].reshape(tokens, D)
            projected = jnp.dot(act_flat, query_table.T, preferred_element_type=jnp.float32)
            running = running + jnp.sum(projected * grad_flat.astype(jnp.float32), axis=1)
        scores.append(running.reshape(SEQS, SEQ_LEN))
    stacked = jnp.stack(scores)
    position = jnp.arange(SEQ_LEN, dtype=jnp.int32)
    valid_mask = position[None, :] < lengths[:, None]
    return jnp.where(valid_mask[None], stacked, 0.0)
```

```python
import functools

import jax
import jax.numpy as jnp
from jax import lax
from jax.experimental import pallas as pl
from jax.experimental.pallas import tpu as pltpu
from jax.sharding import Mesh, PartitionSpec as P

AXES = ("xl", "y", "c", "z", "xh")
SIZES = (2, 8, 2, 8, 2)
NT = (((1,), (1,)), ((), ()))


def transposed_plane():
    xl_n, y_n, c_n, z_n, xh_n = SIZES

    def flat(xl, y, c, z, xh):
        return (((xl * y_n + y) * c_n + c) * z_n + z) * xh_n + xh

    return [
        (flat(xl, y, c, z, xh), flat(xl, z, c, y, xh))
        for xl in range(xl_n)
        for y in range(y_n)
        for c in range(c_n)
        for z in range(z_n)
        for xh in range(xh_n)
    ]


def rotate_kernel(rows_ref, basis_ref, out_ref):
    layers, tokens, _ = rows_ref.shape
    half = tokens // 2
    to = lax.broadcasted_iota(jnp.int32, (tokens, tokens), 0)
    came = lax.broadcasted_iota(jnp.int32, (tokens, tokens), 1)
    wanted = jnp.where(to < half, 2 * to, 2 * (to - half) + 1)
    pick = (came == wanted).astype(jnp.bfloat16)
    for layer in range(layers):
        rows = jnp.dot(pick, rows_ref[layer], preferred_element_type=jnp.float32)
        turned = jnp.dot(
            rows.astype(jnp.bfloat16), basis_ref[layer], preferred_element_type=jnp.float32
        ).astype(jnp.bfloat16)
        for copy in range(out_ref.shape[1]):
            for parity in range(2):
                out_ref[layer, copy, parity] = turned[parity * half:(parity + 1) * half]


def rotate(rows, basis, copies):
    layers, seqs, span, width = rows.shape
    tokens = seqs * span
    return pl.pallas_call(
        rotate_kernel,
        out_shape=jax.ShapeDtypeStruct((layers, copies, 2, tokens // 2, width), jnp.bfloat16),
        cost_estimate=pl.CostEstimate(
            flops=2 * layers * tokens * width * width, bytes_accessed=2 << 20, transcendentals=0
        ),
    )(rows.reshape(layers, tokens, width), basis.reshape(layers, width, width))


def score_kernel(act_ref, grad_ref, table_ref, out_ref):
    owners, blocks, tokens, width = act_ref.shape
    queries = table_ref.shape[2]
    total = owners * tokens
    seqs = tokens // 8
    acts = [act_ref[:, block].reshape(total, width) for block in range(blocks)]
    lane = lax.broadcasted_iota(jnp.int32, (owners, 8, 128), 2)
    out = jnp.zeros((owners, 8, 128), jnp.float32)
    for query in range(queries):
        running = jnp.zeros((total, width), jnp.float32)
        for row_block in range(blocks):
            projected = jnp.zeros((total, width), jnp.float32)
            for block in range(blocks):
                projected += lax.dot_general(
                    acts[block], table_ref[block, row_block, query], NT,
                    preferred_element_type=jnp.float32,
                )
            running += projected * grad_ref[:, row_block].reshape(total, width).astype(jnp.float32)
        column = jnp.sum(running, axis=1, keepdims=True).reshape(owners, seqs, 8, 1)
        for seq in range(seqs):
            out = jnp.where(lane == query * seqs + seq, column[:, seq], out)
    out_ref[...] = out


def score(act, grad, table):
    owners, blocks, tokens, width = act.shape
    queries = table.shape[2]
    return pl.pallas_call(
        score_kernel,
        out_shape=jax.ShapeDtypeStruct((owners, 8, 128), jnp.float32),
        cost_estimate=pl.CostEstimate(
            flops=2 * owners * tokens * queries * (blocks * width) ** 2,
            bytes_accessed=4 << 20,
            transcendentals=0,
        ),
        compiler_params=pltpu.CompilerParams(vmem_limit_bytes=40 << 20),
    )(act, grad, table)


def per_device(act_rows, grad_rows, eig_act, eig_grad, precond, lengths):
    xl_n, y_n, c_n, z_n, xh_n = SIZES
    layers, seqs, span, width = act_rows.shape
    tokens = seqs * span // 2
    table = lax.all_gather(precond, ("c", "xh"), axis=0, tiled=False)
    table = table.reshape((c_n, xh_n) + precond.shape)

    act = rotate(act_rows, eig_act, 1)
    act = lax.ppermute(act, AXES, transposed_plane())
    grad = rotate(grad_rows, eig_grad, y_n)
    grad = lax.all_to_all(
        grad.reshape(xl_n * y_n * xh_n, tokens, width), ("xl", "y", "xh"), 0, 0, tiled=True
    )
    act = jnp.broadcast_to(act, (layers, z_n, 2, tokens, width))
    act = lax.all_to_all(
        act.reshape(xl_n * z_n * xh_n, tokens, width), ("xl", "z", "xh"), 0, 0, tiled=True
    )
    partial_scores = score(
        act.reshape(xl_n * y_n, 2, tokens, width), grad.reshape(xl_n * y_n, 2, tokens, width), table
    )
    shares = lax.all_to_all(
        partial_scores.reshape(xl_n * y_n * z_n, 1, 128), ("xl", "y", "z"), 0, 0, tiled=True
    )
    queries = precond.shape[0]
    summed = jnp.sum(shares, axis=(0, 1))[: queries * seqs].reshape(queries, seqs, 1)
    position = lax.axis_index(("xl", "y", "c", "z", "xh"))
    valid_mask = position < lengths
    return jnp.where(valid_mask[None, :, None], summed, 0.0)


def solution(mesh):
    fine = Mesh(mesh.devices.reshape(SIZES), AXES)
    dp, block = ("xl", "y", "c"), ("z", "xh")
    return jax.shard_map(
        per_device,
        mesh=fine,
        in_specs=(
            P(None, None, dp, block),
            P(None, None, dp, block),
            P(None, block, None, None),
            P(None, block, None, None),
            P(None, block, dp),
            P(),
        ),
        out_specs=P(None, None, dp + block),
        check_vma=False,
    )
```

```python
import jax
import jax.numpy as jnp
from jax import lax
from jax.experimental import pallas as pl
from jax.experimental.pallas import tpu as pltpu
from jax.sharding import Mesh, PartitionSpec as P

AXES = ("xl", "y", "c", "z", "xh")
SIZES = (2, 8, 2, 8, 2)
NT = (((1,), (1,)), ((), ()))


def moved(to):
    _, y_n, c_n, z_n, xh_n = SIZES

    def flat(xl, y, c, z, xh):
        return (((xl * y_n + y) * c_n + c) * z_n + z) * xh_n + xh

    places = [
        (xl, y, c, z, xh)
        for xl in range(SIZES[0])
        for y in range(y_n)
        for c in range(c_n)
        for z in range(z_n)
        for xh in range(xh_n)
    ]
    return [(flat(*place), flat(*to(*place))) for place in places]


def rotate_kernel(act_ref, grad_ref, act_basis_ref, grad_basis_ref, out_ref):
    layers, tokens, _ = act_ref.shape
    half = tokens // 2
    to = lax.broadcasted_iota(jnp.int32, (tokens, tokens), 0)
    came = lax.broadcasted_iota(jnp.int32, (tokens, tokens), 1)
    wanted = jnp.where(to < half, 2 * to, 2 * (to - half) + 1)
    pick = (came == wanted).astype(jnp.bfloat16)
    for layer in range(layers):
        for kind, (rows_ref, basis_ref) in enumerate(
            ((act_ref, act_basis_ref), (grad_ref, grad_basis_ref))
        ):
            rows = jnp.dot(pick, rows_ref[layer], preferred_element_type=jnp.float32)
            turned = jnp.dot(
                rows.astype(jnp.bfloat16), basis_ref[layer], preferred_element_type=jnp.float32
            ).astype(jnp.bfloat16)
            for parity in range(2):
                out_ref[layer, parity, kind] = turned[parity * half:(parity + 1) * half]


def rotate(act_rows, grad_rows, eig_act, eig_grad):
    layers, seqs, span, width = act_rows.shape
    tokens = seqs * span
    rows, basis = (layers, tokens, width), (layers, width, width)
    return pl.pallas_call(
        rotate_kernel,
        out_shape=jax.ShapeDtypeStruct((layers, 2, 2, tokens // 2, width), jnp.bfloat16),
        cost_estimate=pl.CostEstimate(
            flops=4 * layers * tokens * width * width, bytes_accessed=2 << 20, transcendentals=0
        ),
    )(act_rows.reshape(rows), grad_rows.reshape(rows), eig_act.reshape(basis), eig_grad.reshape(basis))


def spread_kernel(rows_ref, *refs):
    out_ref = refs[-1]
    for copy in range(out_ref.shape[0]):
        out_ref[copy] = rows_ref[...]


def spread(rows, copies, after=(), flops=0):
    vmem, anywhere = pl.BlockSpec(memory_space=pltpu.VMEM), pl.BlockSpec(memory_space=pl.ANY)
    return pl.pallas_call(
        spread_kernel,
        out_shape=jax.ShapeDtypeStruct((copies,) + rows.shape, rows.dtype),
        in_specs=[vmem] + [anywhere] * len(after),
        out_specs=vmem,
        cost_estimate=pl.CostEstimate(flops=flops, bytes_accessed=1 << 20, transcendentals=0),
    )(rows, *after)


def score_kernel(place_ref, act_ref, grad_ref, *tables_and_out):
    table_refs, out_ref = tables_and_out[:-1], tables_and_out[-1]
    y_n, xl_n, _, tokens, width = act_ref.shape
    queries = table_refs[0].shape[0]
    seqs = tokens // 8
    total = y_n * tokens
    core, half = place_ref[0], place_ref[1]
    lane = lax.broadcasted_iota(jnp.int32, (y_n, 8, 128), 2)
    for xl in range(xl_n):
        out = jnp.zeros((y_n, 8, 128), jnp.float32)
        acts = [
            act_ref[:, xl, core if n == 0 else 1 - core].reshape(total, width) for n in range(2)
        ]
        grads = [
            grad_ref[:, xl, half if j == 0 else 1 - half].reshape(total, width).astype(jnp.float32)
            for j in range(2)
        ]
        for query in range(queries):
            running = jnp.zeros((total, width), jnp.float32)
            for j in range(2):
                projected = jnp.zeros((total, width), jnp.float32)
                for n in range(2):
                    projected += lax.dot_general(
                        acts[n], table_refs[2 * n + j][query], NT,
                        preferred_element_type=jnp.float32,
                    )
                running += projected * grads[j]
            column = jnp.sum(running, axis=1, keepdims=True).reshape(y_n, seqs, 8, 1)
            for seq in range(seqs):
                out = jnp.where(lane == query * seqs + seq, column[:, seq], out)
        out_ref[:, xl] = out


def score(place, act, grad, tables):
    y_n, xl_n, blocks, tokens, width = act.shape
    queries = tables[0].shape[0]
    vmem = pl.BlockSpec(memory_space=pltpu.VMEM)
    return pl.pallas_call(
        score_kernel,
        out_shape=jax.ShapeDtypeStruct((y_n, xl_n, 8, 128), jnp.float32),
        in_specs=[pl.BlockSpec(memory_space=pltpu.SMEM)] + [vmem] * (2 + len(tables)),
        out_specs=vmem,
        cost_estimate=pl.CostEstimate(
            flops=2 * y_n * xl_n * tokens * queries * (blocks * width) ** 2,
            bytes_accessed=4 << 20,
            transcendentals=0,
        ),
        compiler_params=pltpu.CompilerParams(vmem_limit_bytes=40 << 20),
    )(place, act, grad, *tables)


def per_device(act_rows, grad_rows, eig_act, eig_grad, precond, lengths):
    xl_n, y_n, _, z_n, xh_n = SIZES
    layers, seqs, span, width = act_rows.shape
    queries = precond.shape[0]
    tokens = seqs * span // 2
    place = jnp.stack([lax.axis_index("c"), lax.axis_index("xh")]).astype(jnp.int32)

    turned = rotate(act_rows, grad_rows, eig_act, eig_grad)
    turned = lax.all_to_all(
        turned.reshape(xl_n * xh_n, 2, tokens, width), ("xl", "xh"), 0, 0, tiled=True
    )
    turned, precond = lax.optimization_barrier((turned, precond))
    act = lax.ppermute(turned[:, 0], AXES, moved(lambda xl, y, c, z, xh: (xl, z, c, y, xh)))
    grad = jnp.broadcast_to(turned[:, 1], (y_n, xl_n * xh_n, tokens, width))
    grad = lax.all_to_all(grad, "y", 0, 0, tiled=True)
    other_half = lax.ppermute(precond, "xh", [(0, 1), (1, 0)])
    act = spread(act, z_n, (other_half,), 50_000_000_000)
    act = lax.all_to_all(act, "z", 0, 0, tiled=True)
    swap = [(0, 1), (1, 0)]
    tables = [precond, other_half, lax.ppermute(precond, "c", swap), lax.ppermute(other_half, "c", swap)]
    owners = (y_n, xl_n, xh_n, tokens, width)
    partial_scores = score(place, act.reshape(owners), grad.reshape(owners), tables)
    shares = lax.all_to_all(
        partial_scores.reshape(y_n * xl_n * z_n, 1, 128), ("y", "xl", "z"), 0, 0, tiled=True
    )
    summed = jnp.sum(shares, axis=(0, 1))[: queries * seqs].reshape(queries, seqs, 1)
    position = lax.axis_index(AXES)
    valid_mask = position < lengths
    return jnp.where(valid_mask[None, :, None], summed, 0.0)


def solution(mesh):
    fine = Mesh(mesh.devices.reshape(SIZES), AXES)
    dp, block = ("xl", "y", "c"), ("z", "xh")
    return jax.shard_map(
        per_device,
        mesh=fine,
        in_specs=(
            P(None, None, dp, block),
            P(None, None, dp, block),
            P(None, block, None, None),
            P(None, block, None, None),
            P(None, block, dp),
            P(),
        ),
        out_specs=P(None, None, dp + block),
        check_vma=False,
    )
```

```python
import jax
import jax.numpy as jnp
from jax import lax
from jax.experimental import pallas as pl
from jax.experimental.pallas import tpu as pltpu
from jax.sharding import Mesh, PartitionSpec as P

AXES = ("xl", "y", "c", "z", "xh")
SIZES = (2, 8, 2, 8, 2)
NT = (((1,), (1,)), ((), ()))


def moved(to):
    _, y_n, c_n, z_n, xh_n = SIZES

    def flat(xl, y, c, z, xh):
        return (((xl * y_n + y) * c_n + c) * z_n + z) * xh_n + xh

    places = [
        (xl, y, c, z, xh)
        for xl in range(SIZES[0])
        for y in range(y_n)
        for c in range(c_n)
        for z in range(z_n)
        for xh in range(xh_n)
    ]
    return [(flat(*place), flat(*to(*place))) for place in places]


def rotate_kernel(act_ref, grad_ref, act_basis_ref, grad_basis_ref, out_ref):
    layers, tokens, _ = act_ref.shape
    half = tokens // 2
    to = lax.broadcasted_iota(jnp.int32, (tokens, tokens), 0)
    came = lax.broadcasted_iota(jnp.int32, (tokens, tokens), 1)
    wanted = jnp.where(to < half, 2 * to, 2 * (to - half) + 1)
    pick = (came == wanted).astype(jnp.bfloat16)
    for layer in range(layers):
        for kind, (rows_ref, basis_ref) in enumerate(
            ((act_ref, act_basis_ref), (grad_ref, grad_basis_ref))
        ):
            rows = jnp.dot(pick, rows_ref[layer], preferred_element_type=jnp.float32)
            turned = jnp.dot(
                rows.astype(jnp.bfloat16), basis_ref[layer], preferred_element_type=jnp.float32
            ).astype(jnp.bfloat16)
            for parity in range(2):
                out_ref[layer, parity, kind] = turned[parity * half:(parity + 1) * half]


def rotate(act_rows, grad_rows, eig_act, eig_grad):
    layers, seqs, span, width = act_rows.shape
    tokens = seqs * span
    rows, basis = (layers, tokens, width), (layers, width, width)
    return pl.pallas_call(
        rotate_kernel,
        out_shape=jax.ShapeDtypeStruct((layers, 2, 2, tokens // 2, width), jnp.bfloat16),
        cost_estimate=pl.CostEstimate(
            flops=4 * layers * tokens * width * width, bytes_accessed=2 << 20, transcendentals=0
        ),
    )(act_rows.reshape(rows), grad_rows.reshape(rows), eig_act.reshape(basis), eig_grad.reshape(basis))


def hold_kernel(rows_ref, out_ref):
    pass


def hold(rows):
    anywhere = pl.BlockSpec(memory_space=pl.ANY)
    return pl.pallas_call(
        hold_kernel,
        out_shape=jax.ShapeDtypeStruct(rows.shape, rows.dtype),
        in_specs=[anywhere],
        out_specs=anywhere,
        input_output_aliases={0: 0},
        cost_estimate=pl.CostEstimate(
            flops=50_000_000_000, bytes_accessed=0, transcendentals=0
        ),
    )(rows)


def score_kernel(place_ref, act_ref, grad_ref, *tables_and_out):
    table_refs, out_ref = tables_and_out[:-1], tables_and_out[-1]
    y_n, xl_n, _, tokens, width = act_ref.shape
    queries = table_refs[0].shape[0]
    seqs = tokens // 8
    total = y_n * tokens
    core, half = place_ref[0], place_ref[1]
    lane = lax.broadcasted_iota(jnp.int32, (y_n, 8, 128), 2)
    for xl in range(xl_n):
        out = jnp.zeros((y_n, 8, 128), jnp.float32)
        acts = [
            act_ref[:, xl, core if n == 0 else 1 - core].reshape(total, width) for n in range(2)
        ]
        grads = [
            grad_ref[:, xl, half if j == 0 else 1 - half].reshape(total, width).astype(jnp.float32)
            for j in range(2)
        ]
        for query in range(queries):
            running = jnp.zeros((total, width), jnp.float32)
            for j in range(2):
                projected = jnp.zeros((total, width), jnp.float32)
                for n in range(2):
                    projected += lax.dot_general(
                        acts[n], table_refs[2 * n + j][query], NT,
                        preferred_element_type=jnp.float32,
                    )
                running += projected * grads[j]
            column = jnp.sum(running, axis=1, keepdims=True).reshape(y_n, seqs, 8, 1)
            for seq in range(seqs):
                out = jnp.where(lane == query * seqs + seq, column[:, seq], out)
        out_ref[:, xl] = out


def score(place, act, grad, tables):
    y_n, xl_n, blocks, tokens, width = act.shape
    queries = tables[0].shape[0]
    vmem = pl.BlockSpec(memory_space=pltpu.VMEM)
    return pl.pallas_call(
        score_kernel,
        out_shape=jax.ShapeDtypeStruct((y_n, xl_n, 8, 128), jnp.float32),
        in_specs=[pl.BlockSpec(memory_space=pltpu.SMEM)] + [vmem] * (2 + len(tables)),
        out_specs=vmem,
        cost_estimate=pl.CostEstimate(
            flops=2 * y_n * xl_n * tokens * queries * (blocks * width) ** 2,
            bytes_accessed=4 << 20,
            transcendentals=0,
        ),
        compiler_params=pltpu.CompilerParams(vmem_limit_bytes=40 << 20),
    )(place, act, grad, *tables)


def per_device(act_rows, grad_rows, eig_act, eig_grad, precond, lengths):
    xl_n, y_n, c_n, z_n, xh_n = SIZES
    layers, seqs, span, width = act_rows.shape
    queries = precond.shape[0]
    tokens = seqs * span // 2
    swap = [(0, 1), (1, 0)]
    place = jnp.stack([lax.axis_index("c"), lax.axis_index("xh")]).astype(jnp.int32)
    other_core = lax.ppermute(precond, "c", swap)

    turned = rotate(act_rows, grad_rows, eig_act, eig_grad)
    turned = lax.all_to_all(
        turned.reshape(xl_n * xh_n, 2, tokens, width), ("xl", "xh"), 0, 0, tiled=True
    )
    act = lax.ppermute(turned[:, 0], AXES, moved(lambda xl, y, c, z, xh: (xl, z, c, y, xh)))
    grad = jnp.broadcast_to(turned[:, 1], (y_n, xl_n * xh_n, tokens, width))
    grad = lax.all_to_all(grad, "y", 0, 0, tiled=True)
    act = lax.all_gather(hold(act), "z", axis=0, tiled=False)
    owners = (y_n, xl_n, xh_n, tokens, width)
    tables = [
        precond, lax.ppermute(precond, "xh", swap),
        other_core, lax.ppermute(other_core, "xh", swap),
    ]
    partial_scores = score(place, act.reshape(owners), grad.reshape(owners), tables)
    shares = lax.all_to_all(
        partial_scores.reshape(y_n * xl_n * z_n, 1, 128), ("y", "xl", "z"), 0, 0, tiled=True
    )
    summed = jnp.sum(shares, axis=(0, 1))[: queries * seqs].reshape(queries, seqs, 1)
    position = lax.axis_index(AXES)
    valid_mask = position < lengths
    return jnp.where(valid_mask[None, :, None], summed, 0.0)


def solution(mesh):
    fine = Mesh(mesh.devices.reshape(SIZES), AXES)
    dp, block = ("xl", "y", "c"), ("z", "xh")
    return jax.shard_map(
        per_device,
        mesh=fine,
        in_specs=(
            P(None, None, dp, block),
            P(None, None, dp, block),
            P(None, block, None, None),
            P(None, block, None, None),
            P(None, block, dp),
            P(),
        ),
        out_specs=P(None, None, dp + block),
        check_vma=False,
    )
```

```python
import jax
import jax.numpy as jnp
from jax import lax
from jax.experimental import pallas as pl
from jax.experimental.pallas import tpu as pltpu
from jax.sharding import Mesh, PartitionSpec as P

AXES = ("xl", "y", "c", "z", "xh")
SIZES = (2, 8, 2, 8, 2)
NT = (((1,), (1,)), ((), ()))


def moved(to):
    _, y_n, c_n, z_n, xh_n = SIZES

    def flat(xl, y, c, z, xh):
        return (((xl * y_n + y) * c_n + c) * z_n + z) * xh_n + xh

    places = [
        (xl, y, c, z, xh)
        for xl in range(SIZES[0])
        for y in range(y_n)
        for c in range(c_n)
        for z in range(z_n)
        for xh in range(xh_n)
    ]
    return [(flat(*place), flat(*to(*place))) for place in places]


def rotate_kernel(act_ref, grad_ref, act_basis_ref, grad_basis_ref, out_ref, turned_ref):
    layers, tokens, width = act_ref.shape
    half = tokens // 2
    for layer in range(layers):
        for kind, (rows_ref, basis_ref) in enumerate(
            ((act_ref, act_basis_ref), (grad_ref, grad_basis_ref))
        ):
            turned = jnp.dot(rows_ref[layer], basis_ref[layer], preferred_element_type=jnp.float32)
            for piece in range(turned_ref.shape[2]):
                start, size = 128 * piece, min(128, width - 128 * piece)
                turned_ref[layer, kind, piece, :, :size] = turned[:, start:start + size]
                for parity in range(2):
                    rows = turned_ref[layer, kind, piece, pl.ds(parity, half, 2), :]
                    out_ref[layer, parity, kind, :, start:start + size] = (
                        rows[:, :size].astype(jnp.bfloat16)
                    )


def rotate(act_rows, grad_rows, eig_act, eig_grad):
    layers, seqs, span, width = act_rows.shape
    tokens = seqs * span
    rows, basis = (layers, tokens, width), (layers, width, width)
    return pl.pallas_call(
        rotate_kernel,
        out_shape=jax.ShapeDtypeStruct((layers, 2, 2, tokens // 2, width), jnp.bfloat16),
        scratch_shapes=[pltpu.VMEM((layers, 2, pl.cdiv(width, 128), tokens, 128), jnp.float32)],
        cost_estimate=pl.CostEstimate(
            flops=4 * layers * tokens * width * width, bytes_accessed=2 << 20, transcendentals=0
        ),
    )(act_rows.reshape(rows), grad_rows.reshape(rows), eig_act.reshape(basis), eig_grad.reshape(basis))


def hold_kernel(rows_ref, out_ref):
    pass


def hold(rows):
    anywhere = pl.BlockSpec(memory_space=pl.ANY)
    return pl.pallas_call(
        hold_kernel,
        out_shape=jax.ShapeDtypeStruct(rows.shape, rows.dtype),
        in_specs=[anywhere],
        out_specs=anywhere,
        input_output_aliases={0: 0},
        cost_estimate=pl.CostEstimate(
            flops=50_000_000_000, bytes_accessed=0, transcendentals=0
        ),
    )(rows)


def score_kernel(place_ref, act_ref, grad_ref, *tables_and_out):
    table_refs, out_ref = tables_and_out[:-1], tables_and_out[-1]
    y_n, xl_n, _, tokens, width = act_ref.shape
    queries = table_refs[0].shape[0]
    seqs = tokens // 8
    total = y_n * tokens
    core, half = place_ref[0], place_ref[1]
    lane = lax.broadcasted_iota(jnp.int32, (y_n, 8, 128), 2)
    for xl in range(xl_n):
        out = jnp.zeros((y_n, 8, 128), jnp.float32)
        acts = [
            act_ref[:, xl, core if n == 0 else 1 - core].reshape(total, width) for n in range(2)
        ]
        grads = [
            grad_ref[:, xl, half if j == 0 else 1 - half].reshape(total, width).astype(jnp.float32)
            for j in range(2)
        ]
        for query in range(queries):
            running = jnp.zeros((total, width), jnp.float32)
            for j in range(2):
                projected = jnp.zeros((total, width), jnp.float32)
                for n in range(2):
                    projected += lax.dot_general(
                        acts[n], table_refs[2 * n + j][query], NT,
                        preferred_element_type=jnp.float32,
                    )
                running += projected * grads[j]
            column = jnp.sum(running, axis=1, keepdims=True).reshape(y_n, seqs, 8, 1)
            for seq in range(seqs):
                out = jnp.where(lane == query * seqs + seq, column[:, seq], out)
        out_ref[:, xl] = out


def score(place, act, grad, tables):
    y_n, xl_n, blocks, tokens, width = act.shape
    queries = tables[0].shape[0]
    vmem = pl.BlockSpec(memory_space=pltpu.VMEM)
    return pl.pallas_call(
        score_kernel,
        out_shape=jax.ShapeDtypeStruct((y_n, xl_n, 8, 128), jnp.float32),
        in_specs=[pl.BlockSpec(memory_space=pltpu.SMEM)] + [vmem] * (2 + len(tables)),
        out_specs=vmem,
        cost_estimate=pl.CostEstimate(
            flops=2 * y_n * xl_n * tokens * queries * (blocks * width) ** 2,
            bytes_accessed=4 << 20,
            transcendentals=0,
        ),
        compiler_params=pltpu.CompilerParams(vmem_limit_bytes=40 << 20),
    )(place, act, grad, *tables)


def per_device(act_rows, grad_rows, eig_act, eig_grad, precond, lengths):
    xl_n, y_n, c_n, z_n, xh_n = SIZES
    layers, seqs, span, width = act_rows.shape
    queries = precond.shape[0]
    tokens = seqs * span // 2
    swap = [(0, 1), (1, 0)]
    place = jnp.stack([lax.axis_index("c"), lax.axis_index("xh")]).astype(jnp.int32)
    other_half = lax.ppermute(precond, "xh", swap)

    turned = rotate(act_rows, grad_rows, eig_act, eig_grad)
    turned = lax.all_to_all(
        turned.reshape(xl_n * xh_n, 2, tokens, width), ("xl", "xh"), 0, 0, tiled=True
    )
    act = lax.ppermute(turned[:, 0], AXES, moved(lambda xl, y, c, z, xh: (xl, z, c, y, xh)))
    grad = jnp.broadcast_to(turned[:, 1], (y_n, xl_n * xh_n, tokens, width))
    grad = lax.all_to_all(grad, "y", 0, 0, tiled=True)
    act = lax.all_gather(hold(act), "z", axis=0, tiled=False)
    owners = (y_n, xl_n, xh_n, tokens, width)
    tables = [
        precond, other_half, lax.ppermute(precond, "c", swap), lax.ppermute(other_half, "c", swap),
    ]
    partial_scores = score(place, act.reshape(owners), grad.reshape(owners), tables)
    shares = lax.all_to_all(
        partial_scores.reshape(y_n * xl_n * z_n, 1, 128), ("y", "xl", "z"), 0, 0, tiled=True
    )
    summed = jnp.sum(shares, axis=(0, 1))[: queries * seqs].reshape(queries, seqs, 1)
    position = lax.axis_index(AXES)
    valid_mask = position < lengths
    return jnp.where(valid_mask[None, :, None], summed, 0.0)


def solution(mesh):
    fine = Mesh(mesh.devices.reshape(SIZES), AXES)
    dp, block = ("xl", "y", "c"), ("z", "xh")
    return jax.shard_map(
        per_device,
        mesh=fine,
        in_specs=(
            P(None, None, dp, block),
            P(None, None, dp, block),
            P(None, block, None, None),
            P(None, block, None, None),
            P(None, block, dp),
            P(),
        ),
        out_specs=P(None, None, dp + block),
        check_vma=False,
    )
```

```python
import jax
import jax.numpy as jnp
from jax import lax
from jax.experimental import pallas as pl
from jax.experimental.pallas import tpu as pltpu
from jax.sharding import Mesh, PartitionSpec as P

AXES = ("xl", "y", "c", "z", "xh")
SIZES = (2, 8, 2, 8, 2)


def moved(to):
    _, y_n, c_n, z_n, xh_n = SIZES

    def flat(xl, y, c, z, xh):
        return (((xl * y_n + y) * c_n + c) * z_n + z) * xh_n + xh

    places = [
        (xl, y, c, z, xh)
        for xl in range(SIZES[0])
        for y in range(y_n)
        for c in range(c_n)
        for z in range(z_n)
        for xh in range(xh_n)
    ]
    return [(flat(*place), flat(*to(*place))) for place in places]


def rotate_kernel(act_ref, grad_ref, act_basis_ref, grad_basis_ref, out_ref, turned_ref):
    layers, tokens, width = act_ref.shape
    half = tokens // 2
    for layer in range(layers):
        for kind, (rows_ref, basis_ref) in enumerate(
            ((act_ref, act_basis_ref), (grad_ref, grad_basis_ref))
        ):
            turned = jnp.dot(rows_ref[layer], basis_ref[layer], preferred_element_type=jnp.float32)
            for piece in range(turned_ref.shape[2]):
                start, size = 128 * piece, min(128, width - 128 * piece)
                turned_ref[layer, kind, piece, :, :size] = turned[:, start:start + size]
                for parity in range(2):
                    rows = turned_ref[layer, kind, piece, pl.ds(parity, half, 2), :]
                    out_ref[layer, parity, kind, :, start:start + size] = (
                        rows[:, :size].astype(jnp.bfloat16)
                    )


def rotate(act_rows, grad_rows, eig_act, eig_grad):
    layers, seqs, span, width = act_rows.shape
    tokens = seqs * span
    rows, basis = (layers, tokens, width), (layers, width, width)
    return pl.pallas_call(
        rotate_kernel,
        out_shape=jax.ShapeDtypeStruct((layers, 2, 2, tokens // 2, width), jnp.bfloat16),
        scratch_shapes=[pltpu.VMEM((layers, 2, pl.cdiv(width, 128), tokens, 128), jnp.float32)],
        cost_estimate=pl.CostEstimate(
            flops=4 * layers * tokens * width * width, bytes_accessed=2 << 20, transcendentals=0
        ),
    )(act_rows.reshape(rows), grad_rows.reshape(rows), eig_act.reshape(basis), eig_grad.reshape(basis))


def hold_kernel(rows_ref, out_ref):
    pass


def hold(rows):
    anywhere = pl.BlockSpec(memory_space=pl.ANY)
    return pl.pallas_call(
        hold_kernel,
        out_shape=jax.ShapeDtypeStruct(rows.shape, rows.dtype),
        in_specs=[anywhere],
        out_specs=anywhere,
        input_output_aliases={0: 0},
        cost_estimate=pl.CostEstimate(
            flops=50_000_000_000, bytes_accessed=0, transcendentals=0
        ),
    )(rows)


def score_kernel(place_ref, act_ref, grad_ref, *tables_and_out):
    table_refs, out_ref = tables_and_out[:-1], tables_and_out[-1]
    y_n, xl_n, _, tokens, width = act_ref.shape
    queries = table_refs[0].shape[0]
    seqs = tokens // 8
    total = y_n * xl_n * tokens
    core, half = place_ref[0], place_ref[1]
    act = jnp.concatenate(
        [act_ref[:, :, block].reshape(total, width) for block in (core, 1 - core)], axis=1
    ).astype(jnp.float32)
    grad = jnp.concatenate(
        [grad_ref[:, :, block].reshape(total, width) for block in (half, 1 - half)], axis=1
    )
    lane = lax.broadcasted_iota(jnp.int32, (y_n, xl_n, 8, 128), 3)
    out = jnp.zeros((y_n, xl_n, 8, 128), jnp.float32)
    for query in range(queries):
        table = jnp.concatenate(
            [
                jnp.concatenate([table_refs[j][query], table_refs[2 + j][query]], axis=1)
                for j in range(2)
            ]
        )
        projected = jnp.dot(grad, table, preferred_element_type=jnp.float32)
        column = jnp.sum(projected * act, axis=1, keepdims=True)
        column = column.reshape(y_n, xl_n, seqs, 8, 1)
        for seq in range(seqs):
            out = jnp.where(lane == query * seqs + seq, column[:, :, seq], out)
    out_ref[...] = out


def score(place, act, grad, tables):
    y_n, xl_n, blocks, tokens, width = act.shape
    queries = tables[0].shape[0]
    vmem = pl.BlockSpec(memory_space=pltpu.VMEM)
    return pl.pallas_call(
        score_kernel,
        out_shape=jax.ShapeDtypeStruct((y_n, xl_n, 8, 128), jnp.float32),
        in_specs=[pl.BlockSpec(memory_space=pltpu.SMEM)] + [vmem] * (2 + len(tables)),
        out_specs=vmem,
        cost_estimate=pl.CostEstimate(
            flops=2 * y_n * xl_n * tokens * queries * (blocks * width) ** 2,
            bytes_accessed=4 << 20,
            transcendentals=0,
        ),
        compiler_params=pltpu.CompilerParams(vmem_limit_bytes=40 << 20),
    )(place, act, grad, *tables)


def per_device(act_rows, grad_rows, eig_act, eig_grad, precond, lengths):
    xl_n, y_n, c_n, z_n, xh_n = SIZES
    layers, seqs, span, width = act_rows.shape
    queries = precond.shape[0]
    tokens = seqs * span // 2
    swap = [(0, 1), (1, 0)]
    place = jnp.stack([lax.axis_index("c"), lax.axis_index("xh")]).astype(jnp.int32)
    other_half = lax.ppermute(precond, "xh", swap)

    turned = rotate(act_rows, grad_rows, eig_act, eig_grad)
    turned = lax.all_to_all(
        turned.reshape(xl_n * xh_n, 2, tokens, width), ("xl", "xh"), 0, 0, tiled=True
    )
    act = lax.ppermute(turned[:, 0], AXES, moved(lambda xl, y, c, z, xh: (xl, z, c, y, xh)))
    grad = jnp.broadcast_to(turned[:, 1], (y_n, xl_n * xh_n, tokens, width))
    grad = lax.all_to_all(grad, "y", 0, 0, tiled=True)
    act = lax.all_gather(hold(act), "z", axis=0, tiled=False)
    owners = (y_n, xl_n, xh_n, tokens, width)
    tables = [
        precond, other_half, lax.ppermute(precond, "c", swap), lax.ppermute(other_half, "c", swap),
    ]
    partial_scores = score(place, act.reshape(owners), grad.reshape(owners), tables)
    shares = lax.all_to_all(
        partial_scores.reshape(y_n * xl_n * z_n, 1, 128), ("y", "xl", "z"), 0, 0, tiled=True
    )
    summed = jnp.sum(shares, axis=(0, 1))[: queries * seqs].reshape(queries, seqs, 1)
    position = lax.axis_index(AXES)
    valid_mask = position < lengths
    return jnp.where(valid_mask[None, :, None], summed, 0.0)


def solution(mesh):
    fine = Mesh(mesh.devices.reshape(SIZES), AXES)
    dp, block = ("xl", "y", "c"), ("z", "xh")
    return jax.shard_map(
        per_device,
        mesh=fine,
        in_specs=(
            P(None, None, dp, block),
            P(None, None, dp, block),
            P(None, block, None, None),
            P(None, block, None, None),
            P(None, block, dp),
            P(),
        ),
        out_specs=P(None, None, dp + block),
        check_vma=False,
    )
```

```python
import jax
import jax.numpy as jnp
from jax import lax
from jax.experimental import pallas as pl
from jax.experimental.pallas import tpu as pltpu
from jax.sharding import Mesh, PartitionSpec as P

AXES = ("xl", "y", "c", "z", "xh")
SIZES = (2, 8, 2, 8, 2)


def moved(to):
    _, y_n, c_n, z_n, xh_n = SIZES

    def flat(xl, y, c, z, xh):
        return (((xl * y_n + y) * c_n + c) * z_n + z) * xh_n + xh

    places = [
        (xl, y, c, z, xh)
        for xl in range(SIZES[0])
        for y in range(y_n)
        for c in range(c_n)
        for z in range(z_n)
        for xh in range(xh_n)
    ]
    return [(flat(*place), flat(*to(*place))) for place in places]


def rotate_kernel(act_ref, grad_ref, act_basis_ref, grad_basis_ref, out_ref, turned_ref):
    layers, tokens, width = act_ref.shape
    half = tokens // 2
    for layer in range(layers):
        for kind, (rows_ref, basis_ref) in enumerate(
            ((act_ref, act_basis_ref), (grad_ref, grad_basis_ref))
        ):
            turned = jnp.dot(rows_ref[layer], basis_ref[layer], preferred_element_type=jnp.float32)
            for piece in range(turned_ref.shape[2]):
                start, size = 128 * piece, min(128, width - 128 * piece)
                turned_ref[layer, kind, piece, :, :size] = turned[:, start:start + size]
                for parity in range(2):
                    rows = turned_ref[layer, kind, piece, pl.ds(parity, half, 2), :]
                    out_ref[layer, parity, kind, :, start:start + size] = (
                        rows[:, :size].astype(jnp.bfloat16)
                    )


def rotate(act_rows, grad_rows, eig_act, eig_grad):
    layers, seqs, span, width = act_rows.shape
    tokens = seqs * span
    rows, basis = (layers, tokens, width), (layers, width, width)
    return pl.pallas_call(
        rotate_kernel,
        out_shape=jax.ShapeDtypeStruct((layers, 2, 2, tokens // 2, width), jnp.bfloat16),
        scratch_shapes=[pltpu.VMEM((layers, 2, pl.cdiv(width, 128), tokens, 128), jnp.float32)],
        cost_estimate=pl.CostEstimate(
            flops=4 * layers * tokens * width * width, bytes_accessed=2 << 20, transcendentals=0
        ),
    )(act_rows.reshape(rows), grad_rows.reshape(rows), eig_act.reshape(basis), eig_grad.reshape(basis))


def hold_kernel(rows_ref, out_ref):
    pass


def hold(rows):
    anywhere = pl.BlockSpec(memory_space=pl.ANY)
    return pl.pallas_call(
        hold_kernel,
        out_shape=jax.ShapeDtypeStruct(rows.shape, rows.dtype),
        in_specs=[anywhere],
        out_specs=anywhere,
        input_output_aliases={0: 0},
        cost_estimate=pl.CostEstimate(
            flops=50_000_000_000, bytes_accessed=0, transcendentals=0
        ),
    )(rows)


def score_kernel(place_ref, act_ref, grad_ref, *tables_and_out):
    table_refs, out_ref = tables_and_out[:-1], tables_and_out[-1]
    y_n, xl_n, _, tokens, width = act_ref.shape
    queries = table_refs[0].shape[0]
    seqs = tokens // 8
    total = y_n * xl_n * tokens
    core, half, row = place_ref[0], place_ref[1], place_ref[2]
    places = [lax.rem(2 * row + y_n + y_n // 2 - y, y_n) for y in range(y_n)]
    act = jnp.concatenate(
        [
            jnp.concatenate([act_ref[place, :, block] for place in places]).reshape(total, width)
            for block in (core, 1 - core)
        ],
        axis=1,
    ).astype(jnp.float32)
    grad = jnp.concatenate(
        [grad_ref[:, :, block].reshape(total, width) for block in (half, 1 - half)], axis=1
    )
    lane = lax.broadcasted_iota(jnp.int32, (y_n, xl_n, 8, 128), 3)
    out = jnp.zeros((y_n, xl_n, 8, 128), jnp.float32)
    for query in range(queries):
        table = jnp.concatenate(
            [
                jnp.concatenate([table_refs[j][query], table_refs[2 + j][query]], axis=1)
                for j in range(2)
            ]
        )
        projected = jnp.dot(grad, table, preferred_element_type=jnp.float32)
        column = jnp.sum(projected * act, axis=1, keepdims=True)
        column = column.reshape(y_n, xl_n, seqs, 8, 1)
        for seq in range(seqs):
            out = jnp.where(lane == query * seqs + seq, column[:, :, seq], out)
    length = jnp.full(out.shape, place_ref[3])
    for seq in range(1, seqs):
        length = jnp.where(lax.rem(lane, seqs) == seq, place_ref[3 + seq], length)
    y, xl, z = (lax.broadcasted_iota(jnp.int32, out.shape, axis) for axis in range(3))
    position = ((xl * y_n + y) * 2 + core) * 16 + z * 2 + half
    out_ref[...] = jnp.where(position < length, out, 0.0)


def score(place, act, grad, tables):
    y_n, xl_n, blocks, tokens, width = act.shape
    queries = tables[0].shape[0]
    vmem = pl.BlockSpec(memory_space=pltpu.VMEM)
    return pl.pallas_call(
        score_kernel,
        out_shape=jax.ShapeDtypeStruct((y_n, xl_n, 8, 128), jnp.float32),
        in_specs=[pl.BlockSpec(memory_space=pltpu.SMEM)] + [vmem] * (2 + len(tables)),
        out_specs=vmem,
        cost_estimate=pl.CostEstimate(
            flops=2 * y_n * xl_n * tokens * queries * (blocks * width) ** 2,
            bytes_accessed=4 << 20,
            transcendentals=0,
        ),
        compiler_params=pltpu.CompilerParams(vmem_limit_bytes=40 << 20),
    )(place, act, grad, *tables)


def per_device(act_rows, grad_rows, eig_act, eig_grad, precond, lengths):
    xl_n, y_n, c_n, z_n, xh_n = SIZES
    layers, seqs, span, width = act_rows.shape
    queries = precond.shape[0]
    tokens = seqs * span // 2
    swap = [(0, 1), (1, 0)]
    place = jnp.stack([lax.axis_index(axis) for axis in ("c", "xh", "y")]).astype(jnp.int32)
    place = jnp.concatenate([place, lengths])
    other_half = lax.ppermute(precond, "xh", swap)

    turned = rotate(act_rows, grad_rows, eig_act, eig_grad)
    turned = lax.all_to_all(
        turned.reshape(xl_n * xh_n, 2, tokens, width), ("xl", "xh"), 0, 0, tiled=True
    )
    act = lax.ppermute(
        turned[:, 0], AXES,
        moved(lambda xl, y, c, z, xh: (xl, z, c, (2 * z + z_n // 2 - y) % z_n, xh)),
    )
    grad = jnp.broadcast_to(turned[:, 1], (y_n, xl_n * xh_n, tokens, width))
    grad = lax.all_to_all(grad, "y", 0, 0, tiled=True)
    act = lax.all_gather(hold(act), "z", axis=0, tiled=False)
    owners = (y_n, xl_n, xh_n, tokens, width)
    tables = [
        precond, other_half, lax.ppermute(precond, "c", swap), lax.ppermute(other_half, "c", swap),
    ]
    partial_scores = score(place, act.reshape(owners), grad.reshape(owners), tables)
    shares = lax.all_to_all(
        partial_scores.reshape(y_n * xl_n * z_n, 1, 128), ("y", "xl", "z"), 0, 0, tiled=True
    )
    return jnp.sum(shares, axis=(0, 1))[: queries * seqs].reshape(queries, seqs, 1)


def solution(mesh):
    fine = Mesh(mesh.devices.reshape(SIZES), AXES)
    dp, block = ("xl", "y", "c"), ("z", "xh")
    return jax.shard_map(
        per_device,
        mesh=fine,
        in_specs=(
            P(None, None, dp, block),
            P(None, None, dp, block),
            P(None, block, None, None),
            P(None, block, None, None),
            P(None, block, dp),
            P(),
        ),
        out_specs=P(None, None, dp + block),
        check_vma=False,
    )
```

```python
import jax
import jax.numpy as jnp
from jax import lax
from jax.experimental import pallas as pl
from jax.experimental.pallas import tpu as pltpu
from jax.sharding import Mesh, PartitionSpec as P

AXES = ("xl", "y", "c", "z", "xh")
SIZES = (2, 8, 2, 8, 2)


def moved(to):
    _, y_n, c_n, z_n, xh_n = SIZES

    def flat(xl, y, c, z, xh):
        return (((xl * y_n + y) * c_n + c) * z_n + z) * xh_n + xh

    places = [
        (xl, y, c, z, xh)
        for xl in range(SIZES[0])
        for y in range(y_n)
        for c in range(c_n)
        for z in range(z_n)
        for xh in range(xh_n)
    ]
    return [(flat(*place), flat(*to(*place))) for place in places]


def rotate_kernel(act_ref, grad_ref, act_basis_ref, grad_basis_ref, out_ref, turned_ref):
    layers, tokens, width = act_ref.shape
    half = tokens // 2
    for layer in range(layers):
        for kind, (rows_ref, basis_ref) in enumerate(
            ((act_ref, act_basis_ref), (grad_ref, grad_basis_ref))
        ):
            turned = jnp.dot(rows_ref[layer], basis_ref[layer], preferred_element_type=jnp.float32)
            for piece in range(turned_ref.shape[2]):
                start, size = 128 * piece, min(128, width - 128 * piece)
                turned_ref[layer, kind, piece, :, :size] = turned[:, start:start + size]
                for parity in range(2):
                    rows = turned_ref[layer, kind, piece, pl.ds(parity, half, 2), :]
                    out_ref[layer, parity, kind, :, start:start + size] = (
                        rows[:, :size].astype(jnp.bfloat16)
                    )


def rotate(act_rows, grad_rows, eig_act, eig_grad):
    layers, seqs, span, width = act_rows.shape
    tokens = seqs * span
    rows, basis = (layers, tokens, width), (layers, width, width)
    return pl.pallas_call(
        rotate_kernel,
        out_shape=jax.ShapeDtypeStruct((layers, 2, 2, tokens // 2, width), jnp.bfloat16),
        scratch_shapes=[pltpu.VMEM((layers, 2, pl.cdiv(width, 128), tokens, 128), jnp.float32)],
        cost_estimate=pl.CostEstimate(
            flops=4 * layers * tokens * width * width, bytes_accessed=2 << 20, transcendentals=0
        ),
    )(act_rows.reshape(rows), grad_rows.reshape(rows), eig_act.reshape(basis), eig_grad.reshape(basis))


def hold_kernel(rows_ref, out_ref):
    pass


def hold(rows):
    anywhere = pl.BlockSpec(memory_space=pl.ANY)
    return pl.pallas_call(
        hold_kernel,
        out_shape=jax.ShapeDtypeStruct(rows.shape, rows.dtype),
        in_specs=[anywhere],
        out_specs=anywhere,
        input_output_aliases={0: 0},
        cost_estimate=pl.CostEstimate(
            flops=50_000_000_000, bytes_accessed=0, transcendentals=0
        ),
    )(rows)


def score_kernel(place_ref, act_ref, grad_ref, *tables_and_out):
    table_refs, out_ref = tables_and_out[:-1], tables_and_out[-1]
    y_n, xl_n, _, tokens, width = act_ref.shape
    queries = table_refs[0].shape[0]
    seqs = tokens // 8
    total = y_n * xl_n * tokens
    core, half = place_ref[0], place_ref[1]
    act = jnp.concatenate(
        [act_ref[:, :, block].reshape(total, width) for block in (core, 1 - core)], axis=1
    ).astype(jnp.float32)
    grad = jnp.concatenate(
        [grad_ref[:, :, block].reshape(total, width) for block in (half, 1 - half)], axis=1
    )
    lane = lax.broadcasted_iota(jnp.int32, (y_n, xl_n, 8, 128), 3)
    out = jnp.zeros((y_n, xl_n, 8, 128), jnp.float32)
    for query in range(queries):
        table = jnp.concatenate(
            [
                jnp.concatenate([table_refs[j][query], table_refs[2 + j][query]], axis=1)
                for j in range(2)
            ]
        )
        projected = jnp.dot(grad, table, preferred_element_type=jnp.float32)
        column = jnp.sum(projected * act, axis=1, keepdims=True)
        column = column.reshape(y_n, xl_n, seqs, 8, 1)
        for seq in range(seqs):
            out = jnp.where(lane == query * seqs + seq, column[:, :, seq], out)
    length = jnp.full(out.shape, place_ref[2])
    for seq in range(1, seqs):
        length = jnp.where(lax.rem(lane, seqs) == seq, place_ref[2 + seq], length)
    y, xl, z = (lax.broadcasted_iota(jnp.int32, out.shape, axis) for axis in range(3))
    position = ((xl * y_n + y) * 2 + core) * 16 + z * 2 + half
    out_ref[...] = jnp.where(position < length, out, 0.0)


def score(place, act, grad, tables):
    y_n, xl_n, blocks, tokens, width = act.shape
    queries = tables[0].shape[0]
    vmem = pl.BlockSpec(memory_space=pltpu.VMEM)
    return pl.pallas_call(
        score_kernel,
        out_shape=jax.ShapeDtypeStruct((y_n, xl_n, 8, 128), jnp.float32),
        in_specs=[pl.BlockSpec(memory_space=pltpu.SMEM)] + [vmem] * (2 + len(tables)),
        out_specs=vmem,
        cost_estimate=pl.CostEstimate(
            flops=2 * y_n * xl_n * tokens * queries * (blocks * width) ** 2,
            bytes_accessed=4 << 20,
            transcendentals=0,
        ),
        compiler_params=pltpu.CompilerParams(vmem_limit_bytes=40 << 20),
    )(place, act, grad, *tables)


def per_device(act_rows, grad_rows, eig_act, eig_grad, precond, lengths):
    xl_n, y_n, c_n, z_n, xh_n = SIZES
    layers, seqs, span, width = act_rows.shape
    queries = precond.shape[0]
    tokens = seqs * span // 2
    swap = [(0, 1), (1, 0)]
    place = jnp.stack([lax.axis_index("c"), lax.axis_index("xh")]).astype(jnp.int32)
    place = jnp.concatenate([place, lengths])
    other_half = lax.ppermute(precond, "xh", swap)

    turned = rotate(act_rows, grad_rows, eig_act, eig_grad)
    turned = lax.all_to_all(
        turned.reshape(xl_n * xh_n, 2, tokens, width), ("xl", "xh"), 0, 0, tiled=True
    )
    act = lax.ppermute(turned[:, 0], AXES, moved(lambda xl, y, c, z, xh: (xl, z, c, y, xh)))
    grad = jnp.broadcast_to(turned[:, 1], (y_n, xl_n * xh_n, tokens, width))
    grad = lax.all_to_all(grad, "y", 0, 0, tiled=True)
    act = lax.all_gather(hold(act), "z", axis=0, tiled=False)
    owners = (y_n, xl_n, xh_n, tokens, width)
    tables = [
        precond, other_half, lax.ppermute(precond, "c", swap), lax.ppermute(other_half, "c", swap),
    ]
    partial_scores = score(place, act.reshape(owners), grad.reshape(owners), tables)
    shares = lax.all_to_all(
        partial_scores.reshape(y_n * xl_n * z_n, 1, 128), ("y", "xl", "z"), 0, 0, tiled=True
    )
    return jnp.sum(shares, axis=(0, 1))[: queries * seqs].reshape(queries, seqs, 1)


def solution(mesh):
    fine = Mesh(mesh.devices.reshape(SIZES), AXES)
    dp, block = ("xl", "y", "c"), ("z", "xh")
    return jax.shard_map(
        per_device,
        mesh=fine,
        in_specs=(
            P(None, None, dp, block),
            P(None, None, dp, block),
            P(None, block, None, None),
            P(None, block, None, None),
            P(None, block, dp),
            P(),
        ),
        out_specs=P(None, None, dp + block),
        check_vma=False,
    )
```

```python
import jax
import jax.numpy as jnp
from jax import lax
from jax.experimental import pallas as pl
from jax.experimental.pallas import tpu as pltpu
from jax.sharding import Mesh, PartitionSpec as P

AXES = ("xl", "y", "c", "z", "xh")
SIZES = (2, 8, 2, 8, 2)


def moved(to):
    _, y_n, c_n, z_n, xh_n = SIZES

    def flat(xl, y, c, z, xh):
        return (((xl * y_n + y) * c_n + c) * z_n + z) * xh_n + xh

    places = [
        (xl, y, c, z, xh)
        for xl in range(SIZES[0])
        for y in range(y_n)
        for c in range(c_n)
        for z in range(z_n)
        for xh in range(xh_n)
    ]
    return [(flat(*place), flat(*to(*place))) for place in places]


def rotate_kernel(act_ref, grad_ref, act_basis_ref, grad_basis_ref, out_ref, turned_ref):
    layers, tokens, width = act_ref.shape
    half = tokens // 2
    for layer in range(layers):
        for kind, (rows_ref, basis_ref) in enumerate(
            ((act_ref, act_basis_ref), (grad_ref, grad_basis_ref))
        ):
            turned = jnp.dot(rows_ref[layer], basis_ref[layer], preferred_element_type=jnp.float32)
            for piece in range(turned_ref.shape[2]):
                start, size = 128 * piece, min(128, width - 128 * piece)
                turned_ref[layer, kind, piece, :, :size] = turned[:, start:start + size]
                for parity in range(2):
                    rows = turned_ref[layer, kind, piece, pl.ds(parity, half, 2), :]
                    out_ref[layer, parity, kind, :, start:start + size] = (
                        rows[:, :size].astype(jnp.bfloat16)
                    )


def rotate(act_rows, grad_rows, eig_act, eig_grad):
    layers, seqs, span, width = act_rows.shape
    tokens = seqs * span
    rows, basis = (layers, tokens, width), (layers, width, width)
    return pl.pallas_call(
        rotate_kernel,
        out_shape=jax.ShapeDtypeStruct((layers, 2, 2, tokens // 2, width), jnp.bfloat16),
        grid=(layers,),
        in_specs=[pl.BlockSpec((1, tokens, width), lambda layer: (layer, 0, 0))] * 2
        + [pl.BlockSpec((1, width, width), lambda layer: (layer, 0, 0))] * 2,
        out_specs=pl.BlockSpec(
            (1, 2, 2, tokens // 2, width), lambda layer: (layer, 0, 0, 0, 0)
        ),
        scratch_shapes=[pltpu.VMEM((1, 2, pl.cdiv(width, 128), tokens, 128), jnp.float32)],
        cost_estimate=pl.CostEstimate(
            flops=4 * layers * tokens * width * width, bytes_accessed=2 << 20, transcendentals=0
        ),
    )(act_rows.reshape(rows), grad_rows.reshape(rows), eig_act.reshape(basis), eig_grad.reshape(basis))


def hold_kernel(rows_ref, out_ref):
    pass


def hold(rows):
    anywhere = pl.BlockSpec(memory_space=pl.ANY)
    return pl.pallas_call(
        hold_kernel,
        out_shape=jax.ShapeDtypeStruct(rows.shape, rows.dtype),
        in_specs=[anywhere],
        out_specs=anywhere,
        input_output_aliases={0: 0},
        cost_estimate=pl.CostEstimate(
            flops=50_000_000_000, bytes_accessed=0, transcendentals=0
        ),
    )(rows)


def score_kernel(place_ref, act_ref, grad_ref, *tables_and_out):
    table_refs, out_ref = tables_and_out[:-1], tables_and_out[-1]
    y_n, xl_n, _, tokens, width = act_ref.shape
    queries = table_refs[0].shape[0]
    seqs = tokens // 8
    total = y_n * xl_n * tokens
    core, half = place_ref[0], place_ref[1]
    act = jnp.concatenate(
        [act_ref[:, :, block].reshape(total, width) for block in (core, 1 - core)], axis=1
    ).astype(jnp.float32)
    grad = jnp.concatenate(
        [grad_ref[:, :, block].reshape(total, width) for block in (half, 1 - half)], axis=1
    )
    lane = lax.broadcasted_iota(jnp.int32, (y_n, xl_n, 8, 128), 3)
    out = jnp.zeros((y_n, xl_n, 8, 128), jnp.float32)
    for query in range(queries):
        table = jnp.concatenate(
            [
                jnp.concatenate([table_refs[j][query], table_refs[2 + j][query]], axis=1)
                for j in range(2)
            ]
        )
        projected = jnp.dot(grad, table, preferred_element_type=jnp.float32)
        column = jnp.sum(projected * act, axis=1, keepdims=True)
        column = column.reshape(y_n, xl_n, seqs, 8, 1)
        for seq in range(seqs):
            out = jnp.where(lane == query * seqs + seq, column[:, :, seq], out)
    length = jnp.full(out.shape, place_ref[2])
    for seq in range(1, seqs):
        length = jnp.where(lax.rem(lane, seqs) == seq, place_ref[2 + seq], length)
    y, xl, z = (lax.broadcasted_iota(jnp.int32, out.shape, axis) for axis in range(3))
    position = ((xl * y_n + y) * 2 + core) * 16 + z * 2 + half
    out_ref[...] = jnp.where(position < length, out, 0.0)


def score(place, act, grad, tables):
    y_n, xl_n, blocks, tokens, width = act.shape
    queries = tables[0].shape[0]
    vmem = pl.BlockSpec(memory_space=pltpu.VMEM)
    return pl.pallas_call(
        score_kernel,
        out_shape=jax.ShapeDtypeStruct((y_n, xl_n, 8, 128), jnp.float32),
        in_specs=[pl.BlockSpec(memory_space=pltpu.SMEM)] + [vmem] * (2 + len(tables)),
        out_specs=vmem,
        cost_estimate=pl.CostEstimate(
            flops=2 * y_n * xl_n * tokens * queries * (blocks * width) ** 2,
            bytes_accessed=4 << 20,
            transcendentals=0,
        ),
        compiler_params=pltpu.CompilerParams(vmem_limit_bytes=40 << 20),
    )(place, act, grad, *tables)


def per_device(act_rows, grad_rows, eig_act, eig_grad, precond, lengths):
    xl_n, y_n, c_n, z_n, xh_n = SIZES
    layers, seqs, span, width = act_rows.shape
    queries = precond.shape[0]
    tokens = seqs * span // 2
    swap = [(0, 1), (1, 0)]
    place = jnp.stack([lax.axis_index("c"), lax.axis_index("xh")]).astype(jnp.int32)
    place = jnp.concatenate([place, lengths])
    other_half = lax.ppermute(precond, "xh", swap)

    turned = rotate(act_rows, grad_rows, eig_act, eig_grad)
    turned = lax.all_to_all(
        turned.reshape(xl_n * xh_n, 2, tokens, width), ("xl", "xh"), 0, 0, tiled=True
    )
    act = lax.ppermute(turned[:, 0], AXES, moved(lambda xl, y, c, z, xh: (xl, z, c, y, xh)))
    grad = jnp.broadcast_to(turned[:, 1], (y_n, xl_n * xh_n, tokens, width))
    grad = lax.all_to_all(grad, "y", 0, 0, tiled=True)
    act = lax.all_gather(hold(act), "z", axis=0, tiled=False)
    owners = (y_n, xl_n, xh_n, tokens, width)
    tables = [
        precond, other_half, lax.ppermute(precond, "c", swap), lax.ppermute(other_half, "c", swap),
    ]
    partial_scores = score(place, act.reshape(owners), grad.reshape(owners), tables)
    shares = lax.all_to_all(
        partial_scores.reshape(y_n * xl_n * z_n, 1, 128), ("y", "xl", "z"), 0, 0, tiled=True
    )
    return jnp.sum(shares, axis=(0, 1))[: queries * seqs].reshape(queries, seqs, 1)


def solution(mesh):
    fine = Mesh(mesh.devices.reshape(SIZES), AXES)
    dp, block = ("xl", "y", "c"), ("z", "xh")
    return jax.shard_map(
        per_device,
        mesh=fine,
        in_specs=(
            P(None, None, dp, block),
            P(None, None, dp, block),
            P(None, block, None, None),
            P(None, block, None, None),
            P(None, block, dp),
            P(),
        ),
        out_specs=P(None, None, dp + block),
        check_vma=False,
    )
```
